32 devices in a mesh: dp: 2 (over x), expert: 16 (over z, y, core).
Axes of the slice: x: 2, y: 2, z: 4, core: 2. Of those that a mesh axis runs over, the one named last changes fastest.
Arguments:
- residual_in: bfloat16 [1024, 2048], P(('dp', 'expert')), may hold values from -6 to 6
- attention_out: bfloat16 [1024, 2048], P(('dp', 'expert')), may hold values from -6 to 6
- out_weight: bfloat16 [2048, 2048], P(None, 'dp'), may hold values from -0.125 to 0.125
- post_gain: float32 [2048], replicated, may hold values from 0.1 to 1.9
- router_weight: bfloat16 [2048, 16], replicated, may hold values from -0.125 to 0.125
- expert_ids: int32 [1024, 6], P(('dp', 'expert')), may hold values from 0 to 15, all different within a row; in each aligned block of 32 rows (0 to 31, 32 to 63, ...) at most 24 rows name the same one
- expert_slot: int32 [16], replicated, may hold values from 0 to 15, each once
- expert_gate_up: bfloat16 [16, 2048, 1408], P('expert', 'dp'), may hold values from -0.125 to 0.125
- expert_down: bfloat16 [16, 704, 2048], P('expert', None, 'dp'), may hold values from -0.21875 to 0.21875
- shared_gate_up: bfloat16 [2048, 2, 2816], P(None, None, 'dp'), may hold values from -0.125 to 0.125
- shared_down: bfloat16 [2816, 2048], P(None, 'dp'), may hold values from -0.109375 to 0.109375
- final_gain: float32 [2048], replicated, may hold values from 0.1 to 1.9
Outputs:
- mixed: bfloat16 [1024, 2048], P(('dp', 'expert'))
The draws below stay inside these ranges and needn't reach their ends.
Inputs may be any that keep to these rules, and one draw needn't show every extreme that they name: `expert_ids`: each row names 6 different experts. In each aligned block of 32 rows (the rows of one device) no expert is named by more than 24 rows, a bound that some block reaches. A permutation: expert e is held in slot expert_slot[e].
All inputs are finite; a program needn't handle non-finite values.
Results may differ from the reference program's by a relative error of at most 0.0069.
Values may be sent and summed in bfloat16 or wider, within the bound.
A program may use at most 64 MiB of HBM per device.

```python
import math
import jax
import jax.numpy as jnp
import numpy as np
from jax import lax

D = 2048
HD = 2048
F = 704
FS = 2816
TOPK = 6
ROW_DEV = 32
EXPERTS = 16
ROW_BLOCKS = 32
ROWS = 1024
CAP = 24


def level_of(key, extent, cuts, low, largest):
    factor_of, own = 1.0, jax.random.fold_in(key, 6)
    for dim, parts in cuts:
        heights = jnp.exp(jax.random.uniform(jax.random.fold_in(own, dim), (parts,), jnp.float32, low / len(cuts), largest / len(cuts)))
        factor_of = factor_of * jnp.repeat(heights, extent[dim] // parts).reshape([-1 if axis == dim else 1 for axis in range(len(extent))])
    return factor_of


def deal_out(stream_key, own, number, rows, amount, top, bound, lean):
    order = jax.random.permutation(stream_key, amount)
    packed, ordinary = portions_of(amount, rows * top, bound, lean, True), portions_of(amount, rows * top, bound, lean, False)
    places = jnp.arange(amount)

    def named(tallies, offset_by):
        used = int((tallies > 0).sum())
        fixed = max(1, used // 4)
        passed = fixed + (places - fixed + offset_by * (used - fixed)) % max(1, amount - fixed)
        return jnp.zeros((amount,), jnp.int32).at[order[jnp.where(places < fixed, places, passed)]].set(jnp.asarray(tallies, jnp.int32))

    tallies = jnp.where(number % 4 == 0, named(packed, number // 4), named(ordinary, number - number // 4 - 1))
    mixed = jax.random.permutation(jax.random.fold_in(own, 3), amount)
    source_of, taker = mixed[0:amount // 2 * 2:2], mixed[1:amount // 2 * 2:2]
    room = jnp.minimum(tallies[source_of] - 1, bound - tallies[taker]) // 2
    room = jnp.where((source_of == order[0]) | (taker == order[0]) | (tallies[taker] == 0), 0, jnp.maximum(room, 0))
    passed = jax.random.randint(jax.random.fold_in(own, 4), (amount // 2,), 0, 1 << 20) % (room + 1)
    tallies = tallies.at[source_of].add(-passed).at[taker].add(passed)
    members = jnp.searchsorted(jnp.cumsum(tallies), jnp.arange(rows * top), side="right").astype(jnp.int32)
    table = members.reshape(top, rows).T
    table = table[jax.random.permutation(jax.random.fold_in(own, 1), rows)]
    offset_by = jax.random.randint(jax.random.fold_in(own, 2), (rows, 1), 0, top)
    return jnp.take_along_axis(table, (jnp.arange(top)[None, :] + offset_by) % top, axis=1)


def portions_of(number_of, total, most, lean, full):
    loads = [(1 << 20) // math.isqrt(standing ** lean) + 1 for standing in range(1, number_of + 1)]
    largest = most if full else min(most, max(-(-total // number_of), total * loads[0] // sum(loads)))
    least = 1 if total - largest >= number_of - 1 else 0
    holding, spare = [largest] + [least] * (number_of - 1), total - largest - least * (number_of - 1)
    while spare > 0:
        candidates = [i for i in range(1, number_of) if holding[i] < largest] or [i for i in range(1, number_of) if holding[i] < most]
        whole, left = sum([loads[i] for i in candidates]), spare
        for i in candidates:
            extra = min(most - holding[i], max(1, left * loads[i] // whole), spare)
            holding[i] = holding[i] + extra
            spare = spare - extra
    return np.array(holding)


def scatter_about(key, shape, scale, most, cuts=(), kind=jnp.bfloat16):
    entries = jax.random.normal(key, shape, jnp.float32) * scale
    if len(cuts) > 0:
        entries = level_of(key, shape, cuts, -0.22, 0.18) * entries
    return jnp.clip(entries, min=-most, max=most).astype(kind)


def setup_inputs(seed: int = 0) -> dict:
    key_of = jax.random.split(jax.random.key(seed), 13)
    residual_in = scatter_about(key_of[0], (ROWS, D), 1.0, 6.0, ((0, 32),))
    attention_out = scatter_about(key_of[1], (ROWS, HD), 1.0, 6.0, ((0, 32),))
    out_weight = scatter_about(key_of[2], (HD, D), HD ** -0.5, 0.125, ((1, 2),))
    post_gain = jnp.clip(1.0 + 0.18 * jax.random.normal(key_of[3], (D,), jnp.float32), 0.1, 1.9)
    router_weight = scatter_about(key_of[4], (D, EXPERTS), D ** -0.5, 0.125)
    expert_ids_keys = jax.random.split(jax.random.fold_in(key_of[5], 1), ROWS // ROW_DEV)
    expert_ids_turns = jax.random.permutation(jax.random.fold_in(key_of[5], 3), ROWS // ROW_DEV)
    expert_ids = jax.vmap(lambda own, number: deal_out(jax.random.fold_in(key_of[5], 2), own, number, ROW_DEV, EXPERTS, TOPK, CAP, 2))(expert_ids_keys, expert_ids_turns).reshape((ROWS, TOPK))
    expert_slot = jax.random.permutation(key_of[6], EXPERTS).astype(jnp.int32)
    expert_gate_up = scatter_about(key_of[7], (EXPERTS, D, 2 * F), D ** -0.5, 0.125, ((0, 16), (1, 2)))
    expert_down = scatter_about(key_of[8], (EXPERTS, F, D), F ** -0.5, 0.21875, ((0, 16), (2, 2)))
    shared_gate_up = scatter_about(key_of[9], (D, 2, FS), D ** -0.5, 0.125, ((2, 2),))
    shared_down = scatter_about(key_of[10], (FS, D), FS ** -0.5, 0.109375, ((1, 2),))
    final_gain = jnp.clip(1.0 + 0.18 * jax.random.normal(key_of[11], (D,), jnp.float32), 0.1, 1.9)
    return dict(residual_in=residual_in, attention_out=attention_out, out_weight=out_weight, post_gain=post_gain, router_weight=router_weight, expert_ids=expert_ids, expert_slot=expert_slot, expert_gate_up=expert_gate_up, expert_down=expert_down, shared_gate_up=shared_gate_up, shared_down=shared_down, final_gain=final_gain)


EPS = 1e-06

def rms_scale(values, gain):
    values = values.astype(jnp.float32)
    inverse = lax.rsqrt(lax.optimization_barrier(jnp.mean(values * values, axis=-1, keepdims=True)) + EPS)
    return values * inverse * gain

def reference(residual_in, attention_out, out_weight, post_gain, router_weight, expert_ids, expert_slot, expert_gate_up, expert_down, shared_gate_up, shared_down, final_gain):
    proj = jnp.dot(attention_out, out_weight, preferred_element_type=jnp.float32).astype(jnp.bfloat16)
    resid = (residual_in.astype(jnp.float32) + proj.astype(jnp.float32)).astype(jnp.bfloat16)
    normed = rms_scale(resid, post_gain).astype(jnp.bfloat16)
    logits = jnp.dot(normed, router_weight, preferred_element_type=jnp.float32)
    chosen = jnp.take_along_axis(logits, expert_ids, axis=1)
    raised = jnp.exp(chosen)
    gates = raised / lax.optimization_barrier(jnp.sum(raised, axis=1, keepdims=True))
    slots = expert_slot[expert_ids]
    assigned = ROW_DEV * TOPK
    flat_slots = slots.reshape(ROW_BLOCKS, assigned)
    marked = (flat_slots[:, :, None] == jnp.arange(EXPERTS, dtype=jnp.int32)[None, None, :]).astype(jnp.int32)
    before = jnp.cumsum(marked, axis=1) - marked
    position = lax.optimization_barrier(jnp.sum(before * marked, axis=2)).astype(jnp.int32)
    row_of = (jnp.arange(ROWS * TOPK, dtype=jnp.int32) // TOPK).reshape(ROW_BLOCKS, assigned)
    block_of = jnp.broadcast_to(jnp.arange(ROW_BLOCKS, dtype=jnp.int32)[:, None], (ROW_BLOCKS, assigned))
    row_table = jnp.zeros((EXPERTS, ROW_BLOCKS, CAP), jnp.int32).at[flat_slots, block_of, position].set(row_of)
    gate_table = jnp.zeros((EXPERTS, ROW_BLOCKS, CAP), jnp.float32).at[flat_slots, block_of, position].set(gates.reshape(ROW_BLOCKS, assigned))

    def serve(routed, slot):
        picked = row_table[slot].reshape(-1)
        inputs = normed[picked]
        both = jnp.dot(inputs, expert_gate_up[slot], preferred_element_type=jnp.float32)
        active = (jax.nn.silu(both[:, :F]) * both[:, F:]).astype(jnp.bfloat16)
        output = jnp.dot(active, expert_down[slot], preferred_element_type=jnp.float32).astype(jnp.bfloat16)
        weight = gate_table[slot].reshape(-1)
        return (routed.at[picked].add(weight[:, None] * output.astype(jnp.float32)), None)
    routed, _ = lax.scan(serve, jnp.zeros((ROWS, D), jnp.float32), jnp.arange(EXPERTS, dtype=jnp.int32))
    shared_both = jnp.dot(normed, shared_gate_up.reshape(D, 2 * FS), preferred_element_type=jnp.float32)
    shared_active = (jax.nn.silu(shared_both[:, :FS]) * shared_both[:, FS:]).astype(jnp.bfloat16)
    shared_out = jnp.dot(shared_active, shared_down, preferred_element_type=jnp.float32)
    total = resid.astype(jnp.float32) + routed + shared_out
    return rms_scale(total, final_gain).astype(jnp.bfloat16)
```

```python
import jax
import jax.numpy as jnp
from jax import lax
from jax.sharding import PartitionSpec as P

EPS = 1e-06


def rms_scale(values, gain):
    values = values.astype(jnp.float32)
    inverse = lax.rsqrt(jnp.mean(values * values, axis=-1, keepdims=True) + EPS)
    return values * inverse * gain


def general(
    residual_in,
    attention_out,
    out_weight,
    post_gain,
    router_weight,
    expert_ids,
    expert_slot,
    expert_gate_up,
    expert_down,
    shared_gate_up,
    shared_down,
    final_gain,
):
    rows = residual_in.shape[0]
    width = residual_in.shape[1]
    experts = router_weight.shape[1]
    choose = expert_ids.shape[1]
    capacity = max(2, min(rows, 2 * rows * choose // experts))
    proj_cols = jnp.dot(
        lax.all_gather(attention_out, "dp", axis=0, tiled=True),
        out_weight,
        preferred_element_type=jnp.float32,
    ).astype(jnp.bfloat16)
    proj = lax.all_to_all(proj_cols, "dp", split_axis=0, concat_axis=1, tiled=True)
    resid = (residual_in.astype(jnp.float32) + proj.astype(jnp.float32)).astype(jnp.bfloat16)
    normed = rms_scale(resid, post_gain).astype(jnp.bfloat16)
    logits = jnp.dot(normed, router_weight, preferred_element_type=jnp.float32)
    expert_range = jnp.arange(experts, dtype=jnp.int32)
    picked = expert_ids[:, :, None] == expert_range[None, None, :]
    chosen = jnp.sum(jnp.where(picked, logits[:, None, :], 0.0), axis=2)
    raised = jnp.exp(chosen)
    gates = raised / jnp.sum(raised, axis=1, keepdims=True)
    slots = jnp.sum(jnp.where(picked, expert_slot[None, None, :], 0), axis=2).reshape(-1)
    marked = (slots[:, None] == expert_range[None, :]).astype(jnp.int32)
    order = jnp.arange(rows * choose, dtype=jnp.int32)
    earlier = (order[:, None] > order[None, :]).astype(jnp.bfloat16)
    before = jnp.dot(earlier, marked.astype(jnp.bfloat16), preferred_element_type=jnp.float32)
    before = before.astype(jnp.int32)
    position = jnp.sum(before * marked, axis=1)
    target = slots * capacity + position
    placed = target[:, None] == jnp.arange(experts * capacity, dtype=jnp.int32)[None, :]
    select = jnp.any(placed.reshape(rows, choose, experts * capacity), axis=1).astype(jnp.bfloat16)
    outgoing = jnp.einsum("rs,rd->sd", select, normed, preferred_element_type=jnp.float32)
    outgoing = outgoing.astype(jnp.bfloat16).reshape(experts, capacity, width)
    gate_up_all, down_all = (
        lax.all_gather(expert_gate_up, "dp", axis=1, tiled=True),
        lax.all_gather(expert_down, "dp", axis=2, tiled=True),
    )
    gate_up_full = gate_up_all[0]
    down_full = down_all[0]
    hidden_units = gate_up_full.shape[1] // 2
    received = lax.all_to_all(outgoing, "expert", split_axis=0, concat_axis=0, tiled=True)
    sources, count, _ = received.shape
    flat = received.reshape(sources * count, width)
    both = jnp.dot(flat, gate_up_full, preferred_element_type=jnp.float32)
    active = (jax.nn.silu(both[:, :hidden_units]) * both[:, hidden_units:]).astype(jnp.bfloat16)
    result = jnp.dot(active, down_full, preferred_element_type=jnp.float32).astype(jnp.bfloat16)
    result = result.reshape(sources, count, width)
    returned = lax.all_to_all(result, "expert", split_axis=0, concat_axis=0, tiled=True)
    shared_units = shared_gate_up.shape[2]
    shared_pair = shared_gate_up.reshape(width, 2 * shared_units)
    both = jnp.dot(
        lax.all_gather(normed, "dp", axis=0, tiled=True),
        shared_pair,
        preferred_element_type=jnp.float32,
    )
    shared_hidden = (jax.nn.silu(both[:, :shared_units]) * both[:, shared_units:]).astype(
        jnp.bfloat16
    )
    out_cols = jnp.dot(
        lax.all_gather(shared_hidden, "dp", axis=1, tiled=True),
        shared_down,
        preferred_element_type=jnp.float32,
    )
    shared_out = lax.all_to_all(out_cols, "dp", split_axis=0, concat_axis=1, tiled=True)
    back_rows = jnp.take(returned.reshape(experts * capacity, width), target, axis=0)
    back_rows = back_rows.reshape(rows, choose, width).astype(jnp.float32)
    routed = jnp.sum(gates[:, :, None] * back_rows, axis=1)
    total = resid.astype(jnp.float32) + routed + shared_out
    return rms_scale(total, final_gain).astype(jnp.bfloat16)


def pair(
    residual_in,
    attention_out,
    out_weight,
    post_gain,
    router_weight,
    expert_ids,
    expert_slot,
    expert_gate_up,
    expert_down,
    shared_gate_up,
    shared_down,
    final_gain,
):
    swap = [(0, 1), (1, 0)]
    d = lax.axis_index("dp")
    e = lax.axis_index("expert")
    rows, width = residual_in.shape
    experts = router_weight.shape[1]
    half = width // 2
    proj_cols = jnp.dot(
        lax.all_gather(attention_out, "dp", axis=0, tiled=True),
        out_weight,
        preferred_element_type=jnp.float32,
    ).astype(jnp.bfloat16)
    proj = lax.all_to_all(proj_cols, "dp", split_axis=0, concat_axis=1, tiled=True)
    resid = (residual_in.astype(jnp.float32) + proj.astype(jnp.float32)).astype(jnp.bfloat16)
    normed = rms_scale(resid, post_gain).astype(jnp.bfloat16)
    both_rows = lax.all_gather(normed, "dp", axis=0, tiled=True)
    ids = lax.all_gather(expert_ids, "dp", axis=0, tiled=True)
    mine = lax.dynamic_slice_in_dim(both_rows, d * half, half, axis=1)
    every = lax.all_gather(mine, "expert", axis=0, tiled=True)
    logits = jnp.dot(both_rows, router_weight, preferred_element_type=jnp.float32)
    expert_range = jnp.arange(experts, dtype=jnp.int32)
    named = jnp.any(ids[:, :, None] == expert_range[None, None, :], axis=1)
    raised = jnp.where(named, jnp.exp(logits), 0.0)
    gates = raised / jnp.sum(raised, axis=1, keepdims=True)
    gates_all = lax.all_gather(gates, "expert", axis=0, tiled=True)
    here = (expert_slot == e)[None, :]
    gate = jnp.sum(jnp.where(here, gates_all, 0.0), axis=1, keepdims=True)
    units = expert_gate_up.shape[2] // 2
    part = jnp.dot(every, expert_gate_up[0], preferred_element_type=jnp.float32)
    count = part.shape[0] // 2
    other = lax.dynamic_slice_in_dim(part, (1 - d) * count, count).astype(jnp.bfloat16)
    own = lax.dynamic_slice_in_dim(part, d * count, count)
    both = own + lax.ppermute(other, "dp", swap).astype(jnp.float32)
    active = (jax.nn.silu(both[:, :units]) * both[:, units:]).astype(jnp.bfloat16)
    active = lax.all_gather(active, "dp", axis=0, tiled=True)
    result = jnp.dot(active, expert_down[0], preferred_element_type=jnp.float32)
    result = result.astype(jnp.bfloat16).astype(jnp.float32) * gate
    routed = lax.psum_scatter(
        result.astype(jnp.bfloat16), "expert", scatter_dimension=0, tiled=True
    )
    shared_units = shared_gate_up.shape[2]
    shared_pair = shared_gate_up.reshape(width, 2 * shared_units)
    both = jnp.dot(both_rows, shared_pair, preferred_element_type=jnp.float32)
    shared_hidden = (jax.nn.silu(both[:, :shared_units]) * both[:, shared_units:]).astype(
        jnp.bfloat16
    )
    out_cols = jnp.dot(
        lax.all_gather(shared_hidden, "dp", axis=1, tiled=True),
        shared_down,
        preferred_element_type=jnp.float32,
    )
    sums = routed.astype(jnp.float32) + out_cols
    back = lax.all_to_all(sums, "dp", split_axis=0, concat_axis=1, tiled=True)
    total = resid.astype(jnp.float32) + back
    return rms_scale(total, final_gain).astype(jnp.bfloat16)


def solution(mesh):
    in_specs = (
        P(("dp", "expert"), None),
        P(("dp", "expert"), None),
        P(None, "dp"),
        P(),
        P(),
        P(("dp", "expert"), None),
        P(),
        P("expert", "dp", None),
        P("expert", None, "dp"),
        P(None, None, "dp"),
        P(None, "dp"),
        P(),
    )
    out_specs = P(("dp", "expert"), None)
    return jax.shard_map(
        pair if mesh.shape["dp"] == 2 else general, mesh=mesh, in_specs=in_specs, out_specs=out_specs, check_vma=False
    )
```

```python
import functools

import jax
import jax.numpy as jnp
from jax import lax
from jax.experimental import pallas as pl
from jax.experimental.pallas import tpu as pltpu
from jax.sharding import PartitionSpec as P

EPS = 1e-06


def rms_scale(values, gain):
    values = values.astype(jnp.float32)
    inverse = lax.rsqrt(jnp.mean(values * values, axis=-1, keepdims=True) + EPS)
    return values * inverse * gain


def general(
    residual_in,
    attention_out,
    out_weight,
    post_gain,
    router_weight,
    expert_ids,
    expert_slot,
    expert_gate_up,
    expert_down,
    shared_gate_up,
    shared_down,
    final_gain,
):
    rows = residual_in.shape[0]
    width = residual_in.shape[1]
    experts = router_weight.shape[1]
    choose = expert_ids.shape[1]
    capacity = max(2, min(rows, 2 * rows * choose // experts))
    proj_cols = jnp.dot(
        lax.all_gather(attention_out, "dp", axis=0, tiled=True),
        out_weight,
        preferred_element_type=jnp.float32,
    ).astype(jnp.bfloat16)
    proj = lax.all_to_all(proj_cols, "dp", split_axis=0, concat_axis=1, tiled=True)
    resid = (residual_in.astype(jnp.float32) + proj.astype(jnp.float32)).astype(jnp.bfloat16)
    normed = rms_scale(resid, post_gain).astype(jnp.bfloat16)
    logits = jnp.dot(normed, router_weight, preferred_element_type=jnp.float32)
    expert_range = jnp.arange(experts, dtype=jnp.int32)
    picked = expert_ids[:, :, None] == expert_range[None, None, :]
    chosen = jnp.sum(jnp.where(picked, logits[:, None, :], 0.0), axis=2)
    raised = jnp.exp(chosen)
    gates = raised / jnp.sum(raised, axis=1, keepdims=True)
    slots = jnp.sum(jnp.where(picked, expert_slot[None, None, :], 0), axis=2).reshape(-1)
    marked = (slots[:, None] == expert_range[None, :]).astype(jnp.int32)
    order = jnp.arange(rows * choose, dtype=jnp.int32)
    earlier = (order[:, None] > order[None, :]).astype(jnp.bfloat16)
    before = jnp.dot(earlier, marked.astype(jnp.bfloat16), preferred_element_type=jnp.float32)
    before = before.astype(jnp.int32)
    position = jnp.sum(before * marked, axis=1)
    target = slots * capacity + position
    placed = target[:, None] == jnp.arange(experts * capacity, dtype=jnp.int32)[None, :]
    select = jnp.any(placed.reshape(rows, choose, experts * capacity), axis=1).astype(jnp.bfloat16)
    outgoing = jnp.einsum("rs,rd->sd", select, normed, preferred_element_type=jnp.float32)
    outgoing = outgoing.astype(jnp.bfloat16).reshape(experts, capacity, width)
    gate_up_all, down_all = (
        lax.all_gather(expert_gate_up, "dp", axis=1, tiled=True),
        lax.all_gather(expert_down, "dp", axis=2, tiled=True),
    )
    gate_up_full = gate_up_all[0]
    down_full = down_all[0]
    hidden_units = gate_up_full.shape[1] // 2
    received = lax.all_to_all(outgoing, "expert", split_axis=0, concat_axis=0, tiled=True)
    sources, count, _ = received.shape
    flat = received.reshape(sources * count, width)
    both = jnp.dot(flat, gate_up_full, preferred_element_type=jnp.float32)
    active = (jax.nn.silu(both[:, :hidden_units]) * both[:, hidden_units:]).astype(jnp.bfloat16)
    result = jnp.dot(active, down_full, preferred_element_type=jnp.float32).astype(jnp.bfloat16)
    result = result.reshape(sources, count, width)
    returned = lax.all_to_all(result, "expert", split_axis=0, concat_axis=0, tiled=True)
    shared_units = shared_gate_up.shape[2]
    shared_pair = shared_gate_up.reshape(width, 2 * shared_units)
    both = jnp.dot(
        lax.all_gather(normed, "dp", axis=0, tiled=True),
        shared_pair,
        preferred_element_type=jnp.float32,
    )
    shared_hidden = (jax.nn.silu(both[:, :shared_units]) * both[:, shared_units:]).astype(
        jnp.bfloat16
    )
    out_cols = jnp.dot(
        lax.all_gather(shared_hidden, "dp", axis=1, tiled=True),
        shared_down,
        preferred_element_type=jnp.float32,
    )
    shared_out = lax.all_to_all(out_cols, "dp", split_axis=0, concat_axis=1, tiled=True)
    back_rows = jnp.take(returned.reshape(experts * capacity, width), target, axis=0)
    back_rows = back_rows.reshape(rows, choose, width).astype(jnp.float32)
    routed = jnp.sum(gates[:, :, None] * back_rows, axis=1)
    total = resid.astype(jnp.float32) + routed + shared_out
    return rms_scale(total, final_gain).astype(jnp.bfloat16)


GROUPS = 4


def routed_kernel(
    cap,
    block_ref,
    gate_up_ref,
    down_ref,
    out_ref,
    gath,
    own_part,
    part_send,
    part_recv,
    act_send,
    act_recv,
    con,
    core_send,
    core_recv,
    keep,
    y_send,
    y_recv,
    z_send,
    z_recv,
    gz_s,
    gz_r,
    gy_s,
    gy_r,
    gc_s,
    gc_r,
    p_s,
    p_r,
    a_s,
    a_r,
    c_s,
    c_r,
    y_s,
    y_r,
    z_s,
    z_r,
):
    d = lax.axis_index("dp")
    e = lax.axis_index("expert")
    z, y, c = e // 4, (e // 2) % 2, e % 2
    half = gate_up_ref.shape[0]
    units = down_ref.shape[0]
    pair_rows = block_ref.shape[0]
    span = 2 * pair_rows
    taken = 4 * cap
    experts = 16

    def place(zz, yy, cc):
        return zz * 4 + yy * 2 + cc

    x_peer = (1 - d, e)
    y_peer = (d, place(z, 1 - y, c))
    c_peer = (d, place(z, y, 1 - c))

    def z_peer(dz):
        return (d, place((z + dz) % GROUPS, y, c))

    def copy(src, dst, send, recv, device):
        return pltpu.make_async_remote_copy(
            src_ref=src,
            dst_ref=dst,
            send_sem=send,
            recv_sem=recv,
            device_id=device,
            device_id_type=pl.DeviceIdType.MESH,
        )

    barrier = pltpu.get_barrier_semaphore()
    peers = [x_peer, y_peer, c_peer] + [z_peer(k) for k in range(1, GROUPS)]
    for peer in peers:
        pl.semaphore_signal(
            barrier, inc=1, device_id=peer, device_id_type=pl.DeviceIdType.MESH
        )
    gath[z, y, c] = block_ref[...]
    pl.semaphore_wait(barrier, len(peers))

    started = []

    def go(cp):
        cp.start()
        started.append(cp)

    def source(dz):
        return (z + GROUPS - dz) % GROUPS

    def gather_z(dz):
        return copy(
            gath.at[z, y, c], gath.at[z, y, c], gz_s.at[dz], gz_r.at[dz], z_peer(dz)
        )

    def send_yc(dz):
        held = gath.at[source(dz), y, c]
        go(copy(held, held, gy_s.at[dz], gy_r.at[dz], y_peer))
        go(copy(held, held, gc_s.at[dz, 0], gc_r.at[dz, 0], c_peer))

    def landed(slot, recv):
        copy(slot, slot, gz_s.at[0], recv, x_peer).wait_recv()

    def first():
        for dz in (1, 3, 2):
            go(gather_z(dz))
        send_yc(0)

    def arrive_z(dz):
        landed(gath.at[source(dz), y, c], gz_r.at[dz])
        send_yc(dz)

    def arrive(dz):
        far = gath.at[source(dz), 1 - y, c]
        landed(far, gy_r.at[dz])
        go(copy(far, far, gc_s.at[dz, 1], gc_r.at[dz, 1], c_peer))
        landed(gath.at[source(dz), y, 1 - c], gc_r.at[dz, 0])
        landed(gath.at[source(dz), 1 - y, 1 - c], gc_r.at[dz, 1])

    def facts(dz, h):
        lane = lax.broadcasted_iota(jnp.int32, (span, 128), 1)
        aux = gath[source(dz), h, :, :, pl.ds(half, 128)].reshape(span, 128)
        aux = aux.astype(jnp.float32)
        code = jnp.sum(jnp.where(lane == e, aux, 0.0), axis=1, keepdims=True)
        upper = jnp.where(lane == e + experts, aux, 0.0)
        lower = jnp.where(lane == e + 2 * experts, aux, 0.0)
        gate = jnp.sum(upper + lower, axis=1, keepdims=True)
        row = lax.broadcasted_iota(jnp.int32, (span, taken), 0)
        start = (row // (pair_rows // 2)) * cap
        slot = lax.broadcasted_iota(jnp.int32, (span, taken), 1)
        code = code.astype(jnp.int32)
        hit = (code > 0) & (slot - start == code - 1)
        return jnp.where(hit, 1.0, 0.0).astype(jnp.bfloat16), gate

    def partial(dz, h):
        select, _ = facts(dz, h)
        rows = gath[source(dz), h, :, :, pl.ds(0, half)].reshape(span, half)
        packed = lax.dot_general(
            select, rows, (((0,), (0,)), ((), ())), preferred_element_type=jnp.float32
        ).astype(jnp.bfloat16)
        return jnp.dot(packed, gate_up_ref[...], preferred_element_type=jnp.float32)

    def stage_a(dz):
        part_send[dz] = partial(dz, 1 - d).astype(jnp.bfloat16)
        go(copy(part_send.at[dz], part_recv.at[dz], p_s.at[dz], p_r.at[dz], x_peer))
        own_part[dz] = partial(dz, d)

    def stage_b(dz):
        landed(part_recv.at[dz], p_r.at[dz])
        both = own_part[dz] + part_recv[dz].astype(jnp.float32)
        gate, up = both[:, :units], both[:, units:]
        act_send[dz] = (gate / (1.0 + jnp.exp(-gate)) * up).astype(jnp.bfloat16)
        go(copy(act_send.at[dz], act_recv.at[dz], a_s.at[dz], a_r.at[dz], x_peer))
        spread(dz, 0, d, act_send)

    def spread(dz, i, h, held):
        select, gate = facts(dz, h)
        result = jnp.dot(held[dz], down_ref[...], preferred_element_type=jnp.float32)
        result = result.astype(jnp.bfloat16)
        con[...] = gate * jnp.dot(select, result, preferred_element_type=jnp.float32)
        core_send[dz, i] = con[pl.ds((1 - c) * pair_rows, pair_rows), :].astype(jnp.bfloat16)
        go(
            copy(
                core_send.at[dz, i], core_recv.at[dz, i], c_s.at[dz, i], c_r.at[dz, i], c_peer
            )
        )
        keep[dz, i] = con[pl.ds(c * pair_rows, pair_rows), :]

    def stage_c(dz):
        landed(act_recv.at[dz], a_r.at[dz])
        spread(dz, 1, 1 - d, act_recv)

    near = (d + y) % 2

    def stage_r1(dz):
        for i in range(2):
            landed(core_recv.at[dz, i], c_r.at[dz, i])
        away = keep[dz, 1 - near] + core_recv[dz, 1 - near].astype(jnp.float32)
        y_send[dz] = away.astype(jnp.bfloat16)
        go(copy(y_send.at[dz], y_recv.at[dz], y_s.at[dz], y_r.at[dz], y_peer))

    def stage_r2(dz):
        landed(y_recv.at[dz], y_r.at[dz])
        mine = keep[dz, near] + core_recv[dz, near].astype(jnp.float32)
        mine = mine + y_recv[dz].astype(jnp.float32)
        if dz == 0:
            out_ref[...] = mine
        else:
            z_send[dz] = mine.astype(jnp.bfloat16)
            go(
                copy(
                    z_send.at[dz], z_recv.at[dz], z_s.at[dz], z_r.at[dz], z_peer(GROUPS - dz)
                )
            )

    first()
    arrive(0)
    stage_a(0)
    arrive_z(1)
    arrive_z(3)
    arrive(1)
    stage_a(1)
    arrive_z(2)
    arrive(3)
    stage_a(3)
    stage_b(0)
    arrive(2)
    stage_a(2)
    stage_b(1)
    stage_c(0)
    stage_r1(0)
    stage_b(3)
    stage_c(1)
    stage_r2(0)
    stage_r1(1)
    stage_b(2)
    stage_c(3)
    stage_r2(1)
    stage_r1(3)
    stage_c(2)
    stage_r1(2)
    stage_r2(3)
    stage_r2(2)
    for dz in (1, 3, 2):
        landed(z_recv.at[dz], z_r.at[dz])
        out_ref[...] += z_recv[dz].astype(jnp.float32)
    for cp in started:
        cp.wait_send()


def routed_sum(block, gate_up, down, cap):
    pair_rows, wide = block.shape
    half, both = gate_up.shape
    units, cols = down.shape
    taken = 4 * cap
    bf, f32 = jnp.bfloat16, jnp.float32
    dma = pltpu.SemaphoreType.DMA
    vmem = pl.BlockSpec(memory_space=pltpu.VMEM)
    return pl.pallas_call(
        functools.partial(routed_kernel, cap),
        out_shape=jax.ShapeDtypeStruct((pair_rows, cols), f32),
        in_specs=[vmem] * 3,
        out_specs=vmem,
        scratch_shapes=[
            pltpu.VMEM((4, 2, 2, pair_rows, wide), bf),
            pltpu.VMEM((4, taken, both), f32),
            pltpu.VMEM((4, taken, both), bf),
            pltpu.VMEM((4, taken, both), bf),
            pltpu.VMEM((4, taken, units), bf),
            pltpu.VMEM((4, taken, units), bf),
            pltpu.VMEM((2 * pair_rows, cols), f32),
            pltpu.VMEM((4, 2, pair_rows, cols), bf),
            pltpu.VMEM((4, 2, pair_rows, cols), bf),
            pltpu.VMEM((4, 2, pair_rows, cols), f32),
            pltpu.VMEM((4, pair_rows, cols), bf),
            pltpu.VMEM((4, pair_rows, cols), bf),
            pltpu.VMEM((4, pair_rows, cols), bf),
            pltpu.VMEM((4, pair_rows, cols), bf),
        ]
        + [dma((4,))] * 4
        + [dma((4, 2))] * 2
        + [dma((4,))] * 4
        + [dma((4, 2))] * 2
        + [dma((4,))] * 4,
        compiler_params=pltpu.CompilerParams(
            collective_id=0, has_side_effects=True, vmem_limit_bytes=48 * 2**20
        ),
        cost_estimate=pl.CostEstimate(
            flops=2 * 16 * pair_rows * half * both * 2,
            bytes_accessed=2 * (half * both + units * cols),
            transcendentals=0,
        ),
    )(block, gate_up, down)


def pair(
    residual_in,
    attention_out,
    out_weight,
    post_gain,
    router_weight,
    expert_ids,
    expert_slot,
    expert_gate_up,
    expert_down,
    shared_gate_up,
    shared_down,
    final_gain,
):
    d = lax.axis_index("dp")
    rows, width = residual_in.shape
    experts = router_weight.shape[1]
    choose = expert_ids.shape[1]
    cap = max(2, min(rows, 2 * rows * choose // experts))
    half = width // 2
    proj_cols = jnp.dot(
        lax.all_gather(attention_out, "dp", axis=0, tiled=True),
        out_weight,
        preferred_element_type=jnp.float32,
    ).astype(jnp.bfloat16)
    proj = lax.all_to_all(proj_cols, "dp", split_axis=0, concat_axis=1, tiled=True)
    resid = (residual_in.astype(jnp.float32) + proj.astype(jnp.float32)).astype(jnp.bfloat16)
    normed = rms_scale(resid, post_gain).astype(jnp.bfloat16)
    logits = jnp.dot(normed, router_weight, preferred_element_type=jnp.float32)
    expert_range = jnp.arange(experts, dtype=jnp.int32)
    to_slot = expert_slot[:, None] == expert_range[None, :]
    named = jnp.any(expert_ids[:, :, None] == expert_range[None, None, :], axis=1)
    raised = jnp.where(named, jnp.exp(logits), 0.0)
    gates = raised / jnp.sum(raised, axis=1, keepdims=True)
    gates = jnp.sum(jnp.where(to_slot[None], gates[:, :, None], 0.0), axis=1)
    named = jnp.any(named[:, :, None] & to_slot[None], axis=1)
    order = jnp.arange(rows, dtype=jnp.int32)
    upto = (order[:, None] >= order[None, :]).astype(jnp.bfloat16)
    code = jnp.dot(upto, named.astype(jnp.bfloat16), preferred_element_type=jnp.float32)
    code = jnp.where(named, code, 0.0)
    upper = lax.reduce_precision(gates, exponent_bits=8, mantissa_bits=7)
    aux = jnp.concatenate(
        [code, upper, gates - upper, jnp.zeros((rows, 128 - 3 * experts), jnp.float32)], axis=1
    ).astype(jnp.bfloat16)
    everything = lax.all_gather(
        jnp.concatenate([normed, aux], axis=1), "dp", axis=0, tiled=True
    )
    both_rows = everything[:, :width]
    mine = lax.dynamic_slice_in_dim(everything, d * half, half, axis=1)
    block = jnp.concatenate([mine, everything[:, width:]], axis=1)
    routed = routed_sum(block, expert_gate_up[0], expert_down[0], cap)
    shared_units = shared_gate_up.shape[2]
    shared_pair = shared_gate_up.reshape(width, 2 * shared_units)
    both = jnp.dot(both_rows, shared_pair, preferred_element_type=jnp.float32)
    shared_hidden = (jax.nn.silu(both[:, :shared_units]) * both[:, shared_units:]).astype(
        jnp.bfloat16
    )
    out_cols = jnp.dot(
        lax.all_gather(shared_hidden, "dp", axis=1, tiled=True),
        shared_down,
        preferred_element_type=jnp.float32,
    )
    back = lax.all_to_all(routed + out_cols, "dp", split_axis=0, concat_axis=1, tiled=True)
    total = resid.astype(jnp.float32) + back
    return rms_scale(total, final_gain).astype(jnp.bfloat16)


def solution(mesh):
    in_specs = (
        P(("dp", "expert"), None),
        P(("dp", "expert"), None),
        P(None, "dp"),
        P(),
        P(),
        P(("dp", "expert"), None),
        P(),
        P("expert", "dp", None),
        P("expert", None, "dp"),
        P(None, None, "dp"),
        P(None, "dp"),
        P(),
    )
    out_specs = P(("dp", "expert"), None)
    return jax.shard_map(
        pair if dict(mesh.shape) == {"dp": 2, "expert": 16} else general, mesh=mesh, in_specs=in_specs, out_specs=out_specs, check_vma=False
    )
```

```python
import functools

import jax
import jax.numpy as jnp
from jax import lax
from jax.experimental import pallas as pl
from jax.experimental.pallas import tpu as pltpu
from jax.sharding import PartitionSpec as P

EPS = 1e-06


def rms_scale(values, gain):
    values = values.astype(jnp.float32)
    inverse = lax.rsqrt(jnp.mean(values * values, axis=-1, keepdims=True) + EPS)
    return values * inverse * gain


def general(
    residual_in,
    attention_out,
    out_weight,
    post_gain,
    router_weight,
    expert_ids,
    expert_slot,
    expert_gate_up,
    expert_down,
    shared_gate_up,
    shared_down,
    final_gain,
):
    rows = residual_in.shape[0]
    width = residual_in.shape[1]
    experts = router_weight.shape[1]
    choose = expert_ids.shape[1]
    capacity = max(2, min(rows, 2 * rows * choose // experts))
    proj_cols = jnp.dot(
        lax.all_gather(attention_out, "dp", axis=0, tiled=True),
        out_weight,
        preferred_element_type=jnp.float32,
    ).astype(jnp.bfloat16)
    proj = lax.all_to_all(proj_cols, "dp", split_axis=0, concat_axis=1, tiled=True)
    resid = (residual_in.astype(jnp.float32) + proj.astype(jnp.float32)).astype(jnp.bfloat16)
    normed = rms_scale(resid, post_gain).astype(jnp.bfloat16)
    logits = jnp.dot(normed, router_weight, preferred_element_type=jnp.float32)
    expert_range = jnp.arange(experts, dtype=jnp.int32)
    picked = expert_ids[:, :, None] == expert_range[None, None, :]
    chosen = jnp.sum(jnp.where(picked, logits[:, None, :], 0.0), axis=2)
    raised = jnp.exp(chosen)
    gates = raised / jnp.sum(raised, axis=1, keepdims=True)
    slots = jnp.sum(jnp.where(picked, expert_slot[None, None, :], 0), axis=2).reshape(-1)
    marked = (slots[:, None] == expert_range[None, :]).astype(jnp.int32)
    order = jnp.arange(rows * choose, dtype=jnp.int32)
    earlier = (order[:, None] > order[None, :]).astype(jnp.bfloat16)
    before = jnp.dot(earlier, marked.astype(jnp.bfloat16), preferred_element_type=jnp.float32)
    before = before.astype(jnp.int32)
    position = jnp.sum(before * marked, axis=1)
    target = slots * capacity + position
    placed = target[:, None] == jnp.arange(experts * capacity, dtype=jnp.int32)[None, :]
    select = jnp.any(placed.reshape(rows, choose, experts * capacity), axis=1).astype(jnp.bfloat16)
    outgoing = jnp.einsum("rs,rd->sd", select, normed, preferred_element_type=jnp.float32)
    outgoing = outgoing.astype(jnp.bfloat16).reshape(experts, capacity, width)
    gate_up_all, down_all = (
        lax.all_gather(expert_gate_up, "dp", axis=1, tiled=True),
        lax.all_gather(expert_down, "dp", axis=2, tiled=True),
    )
    gate_up_full = gate_up_all[0]
    down_full = down_all[0]
    hidden_units = gate_up_full.shape[1] // 2
    received = lax.all_to_all(outgoing, "expert", split_axis=0, concat_axis=0, tiled=True)
    sources, count, _ = received.shape
    flat = received.reshape(sources * count, width)
    both = jnp.dot(flat, gate_up_full, preferred_element_type=jnp.float32)
    active = (jax.nn.silu(both[:, :hidden_units]) * both[:, hidden_units:]).astype(jnp.bfloat16)
    result = jnp.dot(active, down_full, preferred_element_type=jnp.float32).astype(jnp.bfloat16)
    result = result.reshape(sources, count, width)
    returned = lax.all_to_all(result, "expert", split_axis=0, concat_axis=0, tiled=True)
    shared_units = shared_gate_up.shape[2]
    shared_pair = shared_gate_up.reshape(width, 2 * shared_units)
    both = jnp.dot(
        lax.all_gather(normed, "dp", axis=0, tiled=True),
        shared_pair,
        preferred_element_type=jnp.float32,
    )
    shared_hidden = (jax.nn.silu(both[:, :shared_units]) * both[:, shared_units:]).astype(
        jnp.bfloat16
    )
    out_cols = jnp.dot(
        lax.all_gather(shared_hidden, "dp", axis=1, tiled=True),
        shared_down,
        preferred_element_type=jnp.float32,
    )
    shared_out = lax.all_to_all(out_cols, "dp", split_axis=0, concat_axis=1, tiled=True)
    back_rows = jnp.take(returned.reshape(experts * capacity, width), target, axis=0)
    back_rows = back_rows.reshape(rows, choose, width).astype(jnp.float32)
    routed = jnp.sum(gates[:, :, None] * back_rows, axis=1)
    total = resid.astype(jnp.float32) + routed + shared_out
    return rms_scale(total, final_gain).astype(jnp.bfloat16)


GROUPS = 4


def routed_kernel(
    cap,
    block_ref,
    gate_up_ref,
    down_ref,
    hidden_ref,
    out_ref,
    hidden_out,
    hidden_recv,
    gath,
    own_part,
    part_send,
    part_recv,
    act_send,
    act_recv,
    con,
    core_send,
    core_recv,
    keep,
    y_send,
    y_recv,
    z_send,
    z_recv,
    gz_s,
    gz_r,
    gy_s,
    gy_r,
    gc_s,
    gc_r,
    p_s,
    p_r,
    a_s,
    a_r,
    c_s,
    c_r,
    y_s,
    y_r,
    z_s,
    z_r,
    h_s,
    h_r,
):
    d = lax.axis_index("dp")
    e = lax.axis_index("expert")
    z, y, c = e // 4, (e // 2) % 2, e % 2
    half = gate_up_ref.shape[0]
    units = down_ref.shape[0]
    pair_rows = block_ref.shape[0]
    span = 2 * pair_rows
    taken = 4 * cap
    experts = 16

    def place(zz, yy, cc):
        return zz * 4 + yy * 2 + cc

    x_peer = (1 - d, e)
    y_peer = (d, place(z, 1 - y, c))
    c_peer = (d, place(z, y, 1 - c))

    def z_peer(dz):
        return (d, place((z + dz) % GROUPS, y, c))

    def copy(src, dst, send, recv, device):
        return pltpu.make_async_remote_copy(
            src_ref=src,
            dst_ref=dst,
            send_sem=send,
            recv_sem=recv,
            device_id=device,
            device_id_type=pl.DeviceIdType.MESH,
        )

    barrier = pltpu.get_barrier_semaphore()
    peers = [x_peer, y_peer, c_peer] + [z_peer(k) for k in range(1, GROUPS)]
    for peer in peers:
        pl.semaphore_signal(
            barrier, inc=1, device_id=peer, device_id_type=pl.DeviceIdType.MESH
        )
    gath[z, y, c] = block_ref[...]
    pl.semaphore_wait(barrier, len(peers))

    started = []

    def go(cp):
        cp.start()
        started.append(cp)

    def source(dz):
        return (z + GROUPS - dz) % GROUPS

    def gather_z(dz):
        return copy(
            gath.at[z, y, c], gath.at[z, y, c], gz_s.at[dz], gz_r.at[dz], z_peer(dz)
        )

    def send_yc(dz):
        held = gath.at[source(dz), y, c]
        go(copy(held, held, gy_s.at[dz], gy_r.at[dz], y_peer))
        go(copy(held, held, gc_s.at[dz, 0], gc_r.at[dz, 0], c_peer))

    def landed(slot, recv):
        copy(slot, slot, gz_s.at[0], recv, x_peer).wait_recv()

    def first():
        for dz in (1, 3, 2):
            go(gather_z(dz))
        send_yc(0)

    def arrive_z(dz):
        landed(gath.at[source(dz), y, c], gz_r.at[dz])
        send_yc(dz)

    def arrive(dz):
        far = gath.at[source(dz), 1 - y, c]
        landed(far, gy_r.at[dz])
        go(copy(far, far, gc_s.at[dz, 1], gc_r.at[dz, 1], c_peer))
        landed(gath.at[source(dz), y, 1 - c], gc_r.at[dz, 0])
        landed(gath.at[source(dz), 1 - y, 1 - c], gc_r.at[dz, 1])

    def facts(dz, h):
        lane = lax.broadcasted_iota(jnp.int32, (span, 128), 1)
        aux = gath[source(dz), h, :, :, pl.ds(half, 128)].reshape(span, 128)
        aux = aux.astype(jnp.float32)
        code = jnp.sum(jnp.where(lane == e, aux, 0.0), axis=1, keepdims=True)
        upper = jnp.where(lane == e + experts, aux, 0.0)
        lower = jnp.where(lane == e + 2 * experts, aux, 0.0)
        gate = jnp.sum(upper + lower, axis=1, keepdims=True)
        row = lax.broadcasted_iota(jnp.int32, (span, taken), 0)
        start = (row // (pair_rows // 2)) * cap
        slot = lax.broadcasted_iota(jnp.int32, (span, taken), 1)
        code = code.astype(jnp.int32)
        hit = (code > 0) & (slot - start == code - 1)
        return jnp.where(hit, 1.0, 0.0).astype(jnp.bfloat16), gate

    def partial(dz, h):
        select, _ = facts(dz, h)
        rows = gath[source(dz), h, :, :, pl.ds(0, half)].reshape(span, half)
        packed = lax.dot_general(
            select, rows, (((0,), (0,)), ((), ())), preferred_element_type=jnp.float32
        ).astype(jnp.bfloat16)
        return jnp.dot(packed, gate_up_ref[...], preferred_element_type=jnp.float32)

    def stage_a(dz):
        part_send[dz] = partial(dz, 1 - d).astype(jnp.bfloat16)
        go(copy(part_send.at[dz], part_recv.at[dz], p_s.at[dz], p_r.at[dz], x_peer))
        own_part[dz] = partial(dz, d)

    def stage_b(dz):
        landed(part_recv.at[dz], p_r.at[dz])
        both = own_part[dz] + part_recv[dz].astype(jnp.float32)
        gate, up = both[:, :units], both[:, units:]
        act_send[dz] = (gate / (1.0 + jnp.exp(-gate)) * up).astype(jnp.bfloat16)
        go(copy(act_send.at[dz], act_recv.at[dz], a_s.at[dz], a_r.at[dz], x_peer))
        spread(dz, 0, d, act_send)

    def spread(dz, i, h, held):
        select, gate = facts(dz, h)
        result = jnp.dot(held[dz], down_ref[...], preferred_element_type=jnp.float32)
        result = result.astype(jnp.bfloat16)
        con[...] = gate * jnp.dot(select, result, preferred_element_type=jnp.float32)
        core_send[dz, i] = con[pl.ds((1 - c) * pair_rows, pair_rows), :].astype(jnp.bfloat16)
        go(
            copy(
                core_send.at[dz, i], core_recv.at[dz, i], c_s.at[dz, i], c_r.at[dz, i], c_peer
            )
        )
        keep[dz, i] = con[pl.ds(c * pair_rows, pair_rows), :]

    def stage_c(dz):
        landed(act_recv.at[dz], a_r.at[dz])
        spread(dz, 1, 1 - d, act_recv)

    near = (d + y) % 2

    def stage_r1(dz):
        for i in range(2):
            landed(core_recv.at[dz, i], c_r.at[dz, i])
        away = keep[dz, 1 - near] + core_recv[dz, 1 - near].astype(jnp.float32)
        y_send[dz] = away.astype(jnp.bfloat16)
        go(copy(y_send.at[dz], y_recv.at[dz], y_s.at[dz], y_r.at[dz], y_peer))

    def stage_r2(dz):
        landed(y_recv.at[dz], y_r.at[dz])
        mine = keep[dz, near] + core_recv[dz, near].astype(jnp.float32)
        mine = mine + y_recv[dz].astype(jnp.float32)
        if dz == 0:
            out_ref[...] = mine
        else:
            z_send[dz] = mine.astype(jnp.bfloat16)
            go(
                copy(
                    z_send.at[dz], z_recv.at[dz], z_s.at[dz], z_r.at[dz], z_peer(GROUPS - dz)
                )
            )

    first()
    go(copy(hidden_ref, hidden_recv, h_s.at[0], h_r.at[0], x_peer))
    arrive(0)
    stage_a(0)
    arrive_z(1)
    arrive_z(3)
    arrive(1)
    stage_a(1)
    arrive_z(2)
    arrive(3)
    stage_a(3)
    stage_b(0)
    arrive(2)
    stage_a(2)
    stage_b(1)
    stage_c(0)
    stage_r1(0)
    stage_b(3)
    stage_c(1)
    stage_r2(0)
    stage_r1(1)
    stage_b(2)
    stage_c(3)
    stage_r2(1)
    stage_r1(3)
    stage_c(2)
    stage_r1(2)
    stage_r2(3)
    stage_r2(2)
    for dz in (1, 3, 2):
        landed(z_recv.at[dz], z_r.at[dz])
        out_ref[...] += z_recv[dz].astype(jnp.float32)
    landed(hidden_recv, h_r.at[0])
    hidden_out[d] = hidden_ref[...]
    hidden_out[1 - d] = hidden_recv[...]
    for cp in started:
        cp.wait_send()


def routed_sum(block, gate_up, down, hidden, cap):
    pair_rows, wide = block.shape
    half, both = gate_up.shape
    units, cols = down.shape
    taken = 4 * cap
    bf, f32 = jnp.bfloat16, jnp.float32
    dma = pltpu.SemaphoreType.DMA
    vmem = pl.BlockSpec(memory_space=pltpu.VMEM)
    return pl.pallas_call(
        functools.partial(routed_kernel, cap),
        out_shape=(
            jax.ShapeDtypeStruct((pair_rows, cols), f32),
            jax.ShapeDtypeStruct((2, *hidden.shape), bf),
        ),
        in_specs=[vmem] * 4,
        out_specs=(vmem, vmem),
        scratch_shapes=[
            pltpu.VMEM(hidden.shape, bf),
            pltpu.VMEM((4, 2, 2, pair_rows, wide), bf),
            pltpu.VMEM((4, taken, both), f32),
            pltpu.VMEM((4, taken, both), bf),
            pltpu.VMEM((4, taken, both), bf),
            pltpu.VMEM((4, taken, units), bf),
            pltpu.VMEM((4, taken, units), bf),
            pltpu.VMEM((2 * pair_rows, cols), f32),
            pltpu.VMEM((4, 2, pair_rows, cols), bf),
            pltpu.VMEM((4, 2, pair_rows, cols), bf),
            pltpu.VMEM((4, 2, pair_rows, cols), f32),
            pltpu.VMEM((4, pair_rows, cols), bf),
            pltpu.VMEM((4, pair_rows, cols), bf),
            pltpu.VMEM((4, pair_rows, cols), bf),
            pltpu.VMEM((4, pair_rows, cols), bf),
        ]
        + [dma((4,))] * 4
        + [dma((4, 2))] * 2
        + [dma((4,))] * 4
        + [dma((4, 2))] * 2
        + [dma((4,))] * 4
        + [dma((1,))] * 2,
        compiler_params=pltpu.CompilerParams(
            collective_id=0, has_side_effects=True, vmem_limit_bytes=48 * 2**20
        ),
        cost_estimate=pl.CostEstimate(
            flops=2 * 16 * pair_rows * half * both * 2,
            bytes_accessed=2 * (half * both + units * cols),
            transcendentals=0,
        ),
    )(block, gate_up, down, hidden)


def pair(
    residual_in,
    attention_out,
    out_weight,
    post_gain,
    router_weight,
    expert_ids,
    expert_slot,
    expert_gate_up,
    expert_down,
    shared_gate_up,
    shared_down,
    final_gain,
):
    d = lax.axis_index("dp")
    rows, width = residual_in.shape
    experts = router_weight.shape[1]
    choose = expert_ids.shape[1]
    cap = max(2, min(rows, 2 * rows * choose // experts))
    half = width // 2
    proj_cols = jnp.dot(
        lax.all_gather(attention_out, "dp", axis=0, tiled=True),
        out_weight,
        preferred_element_type=jnp.float32,
    ).astype(jnp.bfloat16)
    proj = lax.all_to_all(proj_cols, "dp", split_axis=0, concat_axis=1, tiled=True)
    resid = (residual_in.astype(jnp.float32) + proj.astype(jnp.float32)).astype(jnp.bfloat16)
    normed = rms_scale(resid, post_gain).astype(jnp.bfloat16)
    logits = jnp.dot(normed, router_weight, preferred_element_type=jnp.float32)
    expert_range = jnp.arange(experts, dtype=jnp.int32)
    to_slot = expert_slot[:, None] == expert_range[None, :]
    named = jnp.any(expert_ids[:, :, None] == expert_range[None, None, :], axis=1)
    raised = jnp.where(named, jnp.exp(logits), 0.0)
    gates = raised / jnp.sum(raised, axis=1, keepdims=True)
    gates = jnp.sum(jnp.where(to_slot[None], gates[:, :, None], 0.0), axis=1)
    named = jnp.any(named[:, :, None] & to_slot[None], axis=1)
    order = jnp.arange(rows, dtype=jnp.int32)
    upto = (order[:, None] >= order[None, :]).astype(jnp.bfloat16)
    code = jnp.dot(upto, named.astype(jnp.bfloat16), preferred_element_type=jnp.float32)
    code = jnp.where(named, code, 0.0)
    upper = lax.reduce_precision(gates, exponent_bits=8, mantissa_bits=7)
    aux = jnp.concatenate(
        [code, upper, gates - upper, jnp.zeros((rows, 128 - 3 * experts), jnp.float32)], axis=1
    ).astype(jnp.bfloat16)
    everything = lax.all_gather(
        jnp.concatenate([normed, aux], axis=1), "dp", axis=0, tiled=True
    )
    both_rows = everything[:, :width]
    mine = lax.dynamic_slice_in_dim(everything, d * half, half, axis=1)
    block = jnp.concatenate([mine, everything[:, width:]], axis=1)
    shared_units = shared_gate_up.shape[2]
    shared_pair = shared_gate_up.reshape(width, 2 * shared_units)
    both = jnp.dot(both_rows, shared_pair, preferred_element_type=jnp.float32)
    shared_hidden = (jax.nn.silu(both[:, :shared_units]) * both[:, shared_units:]).astype(
        jnp.bfloat16
    )
    routed, hidden = routed_sum(
        block, expert_gate_up[0], expert_down[0], shared_hidden, cap
    )
    out_cols = jnp.dot(hidden[0], shared_down[:shared_units], preferred_element_type=jnp.float32)
    out_cols += jnp.dot(hidden[1], shared_down[shared_units:], preferred_element_type=jnp.float32)
    sums = (routed + out_cols).astype(jnp.bfloat16)
    back = lax.all_to_all(sums, "dp", split_axis=0, concat_axis=1, tiled=True)
    total = resid.astype(jnp.float32) + back.astype(jnp.float32)
    return rms_scale(total, final_gain).astype(jnp.bfloat16)


def solution(mesh):
    in_specs = (
        P(("dp", "expert"), None),
        P(("dp", "expert"), None),
        P(None, "dp"),
        P(),
        P(),
        P(("dp", "expert"), None),
        P(),
        P("expert", "dp", None),
        P("expert", None, "dp"),
        P(None, None, "dp"),
        P(None, "dp"),
        P(),
    )
    out_specs = P(("dp", "expert"), None)
    return jax.shard_map(
        pair if dict(mesh.shape) == {"dp": 2, "expert": 16} else general, mesh=mesh, in_specs=in_specs, out_specs=out_specs, check_vma=False
    )
```
